32 devices in a mesh: copies: 2 (over y), blk: 4 (over x, core), virt: 4 (over z).
Axes of the slice: x: 2, y: 2, z: 4, core: 2. Of those that a mesh axis runs over, the one named last changes fastest.
Arguments:
- three_index: bfloat16 [32, 512, 2048], P(('copies', 'blk'), 'virt'), parts along dimension 0, may hold values from -0.59765625 to 0.59765625
- occ_energy: float32 [32], P(('copies', 'blk')), parts along dimension 0, may hold values from -2 to -0.5
- virt_energy: float32 [1024], P('copies'), parts along dimension 0, may hold values from 0.3 to 3
Outputs:
- gradient: bfloat16 [32, 512, 2048], P(('copies', 'blk'), 'virt'), parts along dimension 0
The draws below stay inside these ranges and needn't reach their ends.
There are 2 independent parts, one for each index of `copies`. The reference program is written for one: setup_inputs(seed, part) draws one part's arguments, and reference() takes and returns one part's arrays. A program takes and returns all parts, laid end to end along the dimension named above; each array names one. Nothing has to cross between parts.
All inputs are finite; a program needn't handle non-finite values.
Results may differ from the reference program's by a relative error of at most 0.0055.
Values may be sent and summed in bfloat16 or wider, within the bound.
No kernel may reach another device: no remote copies, remote signals or barrier semaphores. Data moves between devices by JAX's collectives and lax.ppermute only.
A program may use at most 64 MiB of HBM per device.

```python
import jax
import jax.numpy as jnp
from jax import lax

OCC_BLK = 4
VIRT = 512
AUX = 2048
NOCC = 16
N_BLK = 4


def level_of(own_key, shape, cuts, smallest, largest):
    loudness = 1.0
    for position, parts in cuts:
        heights = jax.random.uniform(jax.random.fold_in(jax.random.fold_in(own_key, 6), position), (parts,), jnp.float32, smallest / len(cuts), largest / len(cuts))
        loudness = loudness * jnp.repeat(jnp.exp(heights), shape[position] // parts).reshape((-1,) + (1,) * (len(shape) - 1 - position))
    return loudness


def bell_draw(stream_key, dims, width, reach, cuts=(), kind=jnp.bfloat16):
    drawn = width * jax.random.normal(stream_key, dims, jnp.float32)
    if cuts:
        drawn = drawn * level_of(stream_key, dims, cuts, -0.22, 0.18)
    return jnp.clip(drawn, -reach, reach).astype(kind)


def setup_inputs(seed: int = 0, part: int = 0) -> dict:
    key_list = jax.random.split(jax.random.key(seed), 4)
    own_keys = jax.random.split(jax.random.fold_in(key_list[3], part), 4)
    return {
        "three_index": bell_draw(own_keys[0], (NOCC, VIRT, AUX), 0.1, 0.59765625, ((0, 4), (1, 4))),
        "occ_energy": jnp.clip(-2.0 + 1.5 * jax.random.uniform(own_keys[1], (NOCC,), jnp.float32) ** level_of(own_keys[1], (NOCC,), ((0, 4),), -0.2, 0.2), -2.0, -0.5),
        "virt_energy": jnp.clip(jax.random.uniform(own_keys[2], (VIRT,), jnp.float32, 0.3, 3.0), 0.3, 3.0),
    }


def pair_terms(block_own, block_part, energy_own, energy_part, virt_energy):
    occ_count, virt_count, aux_count = block_own.shape
    first = jnp.dot(block_own.reshape(occ_count * virt_count, aux_count), block_part.reshape(occ_count * virt_count, aux_count).T, preferred_element_type=jnp.float32)
    first = first.reshape(occ_count, virt_count, occ_count, virt_count)
    swapped = first.transpose(0, 3, 2, 1)
    denom = energy_own[:, None, None, None] + energy_part[None, None, :, None] - virt_energy[None, :, None, None] - virt_energy[None, None, None, :]
    tbar = ((2.0 * first - swapped) / denom).astype(jnp.bfloat16)
    flat = tbar.reshape(occ_count * virt_count, occ_count * virt_count)
    own = jnp.dot(flat, block_part.reshape(occ_count * virt_count, aux_count), preferred_element_type=jnp.float32)
    return flat, own.reshape(occ_count, virt_count, aux_count)


def partner_term(flat, block_own):
    occ_count, virt_count, aux_count = block_own.shape
    total = lax.dot_general(flat, block_own.reshape(occ_count * virt_count, aux_count), (((0,), (0,)), ((), ())), preferred_element_type=jnp.float32)
    return total.reshape(occ_count, virt_count, aux_count).astype(jnp.bfloat16)


def reference(three_index, occ_energy, virt_energy):
    owns = []
    partners = []
    for group in range(N_BLK):
        other = (group - 1) % N_BLK
        block_own = three_index[group * OCC_BLK:(group + 1) * OCC_BLK]
        block_part = three_index[other * OCC_BLK:(other + 1) * OCC_BLK]
        energy_own = occ_energy[group * OCC_BLK:(group + 1) * OCC_BLK]
        energy_part = occ_energy[other * OCC_BLK:(other + 1) * OCC_BLK]
        unused, diag_own = pair_terms(block_own, block_own, energy_own, energy_own, virt_energy)
        flat, cross_own = pair_terms(block_own, block_part, energy_own, energy_part, virt_energy)
        owns.append(diag_own + cross_own)
        partners.append(partner_term(flat, block_own))
    blocks = []
    for group in range(N_BLK):
        later = (group + 1) % N_BLK
        blocks.append((owns[group] + partners[later].astype(jnp.float32)).astype(jnp.bfloat16))
    return jnp.concatenate(blocks, axis=0)
```

```python
import functools

import jax
import jax.numpy as jnp
from jax import lax
from jax.experimental import pallas as pl
from jax.experimental.pallas import tpu as pltpu
from jax.sharding import PartitionSpec as P

LANES = 128
VMEM_BYTES = 48 * 2**20


def shifted(shard, axis, by):
    devices = lax.axis_size(axis)
    return lax.ppermute(shard, axis, [(i, (i + by) % devices) for i in range(devices)])


def contract(left, right):
    return lax.dot_general(
        left, right, (((1,), (1,)), ((), ())), preferred_element_type=jnp.float32
    )


def tile_plain(rows, tile, energies, sums, want):
    own_rows, part_rows = rows
    own_tile, part_tile = tile
    energy_own, energy_part, virt_rows, virt_tile = energies
    occ, here, there = energy_own.shape[0], virt_rows.shape[0], virt_tile.shape[0]
    shape = (occ, there, occ, here)
    diag = contract(own_tile, own_rows).reshape(shape)
    first = contract(part_tile, own_rows).reshape(shape)
    second = contract(own_tile, part_rows).reshape(shape)
    virt = virt_tile[None, :, None, None] + virt_rows[None, None, None, :]
    denom_diag = energy_own[:, None, None, None] + energy_own[None, None, :, None] - virt
    denom_cross = energy_part[:, None, None, None] + energy_own[None, None, :, None] - virt
    swap = (2, 1, 0, 3)
    t_diag = ((2.0 * diag - diag.transpose(swap)) / denom_diag).astype(jnp.bfloat16)
    t_cross = ((2.0 * first - second.transpose(swap)) / denom_cross).astype(jnp.bfloat16)
    t_back = ((2.0 * second - first.transpose(swap)) / denom_cross.transpose(swap)).astype(jnp.bfloat16)

    def spread(amplitudes, rows):
        return lax.dot_general(
            amplitudes.reshape(occ * there, occ * here),
            rows,
            (((0,), (0,)), ((), ())),
            preferred_element_type=jnp.float32,
        )

    terms = {
        "own": lambda: spread(t_diag, own_tile) + spread(t_cross, part_tile),
        "partner": lambda: spread(t_back, own_tile),
    }
    return [terms[name]() if total is None else total + terms[name]() for name, total in zip(want, sums)]


def tile_kernel(
    occ, here, there, columns, want, summed, energy_own, energy_part, virt_rows, virt_tile,
    own_rows, part_rows, own_tile, part_tile, *refs,
):
    sums = refs[:len(want)] if summed else (None,) * len(want)
    refs = refs[len(want):] if summed else refs
    outs = refs[:len(want)]
    tiles, gram, first, second, left, sem = refs[len(want):]
    wide = occ * there
    own, partner = "own" in want, "partner" in want
    step = pl.program_id(0)

    @pl.when(step == 0)
    def _():
        copies = [
            pltpu.make_async_copy(own_tile, tiles.at[pl.ds(0, wide)], sem.at[0]),
            pltpu.make_async_copy(part_tile, tiles.at[pl.ds(wide, wide)], sem.at[1]),
        ]
        for copy in copies:
            copy.start()
        copies[0].wait()
        if own:
            gram[...] = contract(tiles[:wide], own_rows[...])
        second[...] = contract(tiles[:wide], part_rows[...])
        copies[1].wait()
        first[...] = contract(tiles[wide:], own_rows[...])
        virt = virt_tile[...] + virt_rows[...]

        def block(ref, r, c):
            return ref[r * there:(r + 1) * there, c * here:(c + 1) * here]

        def place(column, blocks, c):
            left[c * here:(c + 1) * here, column:column + wide] = (
                jnp.concatenate(blocks, axis=0).T.astype(jnp.bfloat16)
            )

        for i in range(occ):
            if own:
                place(0, [
                    (2.0 * block(gram, j, i) - block(gram, i, j)) / (energy_own[i] + energy_own[j] - virt)
                    for j in range(occ)
                ], i)
                place(wide, [
                    (2.0 * block(first, j, i) - block(second, i, j)) / (energy_own[i] + energy_part[j] - virt)
                    for j in range(occ)
                ], i)
        if partner:
            for j in range(occ):
                place(2 * wide if own else 0, [
                    (2.0 * block(second, i, j) - block(first, j, i)) / (energy_own[i] + energy_part[j] - virt)
                    for i in range(occ)
                ], j)

    at = pl.ds(pl.multiple_of(step * columns, columns), columns)
    for name, total, out in zip(want, sums, outs):
        if name == "own":
            term = jnp.dot(left[:, :2 * wide], tiles[:, at], preferred_element_type=jnp.float32)
        else:
            begin = 2 * wide if own else 0
            term = jnp.dot(
                left[:, begin:begin + wide], tiles[pl.ds(0, wide), at], preferred_element_type=jnp.float32
            )
        out[...] = (term if total is None else total[...] + term).astype(out.dtype)


def tile_terms(rows, tile, energies, sums, want, kinds=None):
    energy_own, energy_part, virt_rows, virt_tile = energies
    occ, here, there = energy_own.shape[0], virt_rows.shape[0], virt_tile.shape[0]
    kinds = kinds or (jnp.float32,) * len(want)
    if here % LANES or (occ * there) % LANES or there % 16:
        return [t.astype(k) for t, k in zip(tile_plain(rows, tile, energies, sums, want), kinds)]
    aux = rows[0].shape[1]
    columns = min(aux, 512)
    wide, tall = occ * there, occ * here
    summed = sums[0] is not None
    scalar = pl.BlockSpec(memory_space=pltpu.SMEM)
    whole = lambda shape: pl.BlockSpec(shape, lambda p: (0, 0))
    column = pl.BlockSpec((tall, columns), lambda p: (0, p))
    hbm = pl.BlockSpec(memory_space=pl.ANY)
    products = 3 if "own" in want else 2
    spreads = (2 if "own" in want else 0) + (1 if "partner" in want else 0)
    return pl.pallas_call(
        functools.partial(tile_kernel, occ, here, there, columns, want, summed),
        grid=(aux // columns,),
        in_specs=[
            scalar, scalar, whole((1, here)), whole((there, 1)),
            whole((tall, aux)), whole((tall, aux)), hbm, hbm,
        ] + ([column] * len(want) if summed else []),
        out_specs=[column] * len(want),
        out_shape=[jax.ShapeDtypeStruct((tall, aux), kind) for kind in kinds],
        scratch_shapes=[
            pltpu.VMEM((2 * wide, aux), jnp.bfloat16),
            pltpu.VMEM((wide, tall), jnp.float32),
            pltpu.VMEM((wide, tall), jnp.float32),
            pltpu.VMEM((wide, tall), jnp.float32),
            pltpu.VMEM((tall, spreads * wide), jnp.bfloat16),
            pltpu.SemaphoreType.DMA((2,)),
        ],
        compiler_params=pltpu.CompilerParams(vmem_limit_bytes=VMEM_BYTES),
        cost_estimate=pl.CostEstimate(
            flops=2 * (products + spreads) * wide * tall * aux,
            bytes_accessed=4 * aux * (tall + wide) + 8 * tall * aux * len(want),
            transcendentals=0,
        ),
    )(
        energy_own, energy_part, virt_rows[None, :], virt_tile[:, None],
        *rows, *tile, *(sums if summed else ()),
    )


def local(three_index, occ_energy, virt_energy):
    occ, here, aux = three_index.shape
    steps = lax.axis_size("virt")
    me = lax.axis_index("virt")
    chunks = 2 if here % 64 == 0 else 1
    size = here // chunks
    energy_part = shifted(occ_energy, "blk", 1)
    virt_rows = lax.dynamic_slice_in_dim(virt_energy, me * here, here, 0)
    own_rows = three_index.reshape(occ * here, aux)
    part_rows = shifted(own_rows, "blk", 1)

    def cut(rows, c):
        return rows.reshape(occ, here, aux)[:, c * size:(c + 1) * size].reshape(occ * size, aux)

    tiles = [cut(own_rows, c) for c in range(chunks)]
    parts = [cut(part_rows, c) for c in range(chunks)]
    rows = (own_rows, part_rows)
    sums = (None, None)
    both = ("own", "partner")
    for step in range(steps):
        later = [shifted(tile, "virt", 1) for tile in tiles] if step < steps - 1 else None
        if step:
            parts = [shifted(tile, "blk", 1) for tile in tiles]
        start = lax.rem(me - step + steps, steps) * here
        for c in range(chunks):
            virt_tile = lax.dynamic_slice_in_dim(virt_energy, start + c * size, size, 0)
            energies = (occ_energy, energy_part, virt_rows, virt_tile)
            tile = (tiles[c], parts[c])
            if step == steps - 1 and c == chunks - 1:
                partner, = tile_terms(rows, tile, energies, sums[1:], ("partner",), (jnp.bfloat16,))
                back = shifted(partner, "blk", -1)
                own, = tile_terms(rows, tile, energies, sums[:1], ("own",))
            else:
                sums = tile_terms(rows, tile, energies, sums, both)
        tiles = later
    return (own + back.astype(jnp.float32)).astype(jnp.bfloat16).reshape(occ, here, aux)


def solution(mesh):
    placed = (P(("copies", "blk"), "virt", None), P(("copies", "blk")), P("copies"))
    return jax.shard_map(
        local,
        mesh=mesh,
        in_specs=placed,
        out_specs=P(("copies", "blk"), "virt", None),
        check_vma=False,
    )
```

```python
import functools

import jax
import jax.numpy as jnp
from jax import lax
from jax.experimental import pallas as pl
from jax.experimental.pallas import tpu as pltpu
from jax.sharding import PartitionSpec as P

LANES = 128
VMEM_BYTES = 32 * 2**20


def shifted(shard, axis, by):
    devices = lax.axis_size(axis)
    return lax.ppermute(shard, axis, [(i, (i + by) % devices) for i in range(devices)])


def around(shard, odd):
    groups, devices = lax.axis_size("blk"), lax.axis_size("virt")
    return lax.ppermute(shard, ("blk", "virt"), [
        (g * devices + i, g * devices + (i + 1) % devices)
        for g in range(odd, groups, 2)
        for i in range(devices)
    ])


def passed(shard, odd, by):
    groups = lax.axis_size("blk")
    return lax.ppermute(shard, "blk", [(g, (g + by) % groups) for g in range(odd, groups, 2)])


def in_odd_group():
    return lax.rem(lax.axis_index("blk"), 2) == 1


def contract(left, right):
    return lax.dot_general(
        left, right, (((1,), (1,)), ((), ())), preferred_element_type=jnp.float32
    )


def first_row(span, here):
    step, begin = span
    steps = lax.axis_size("virt")
    return lax.rem(lax.axis_index("virt") + (steps - step), steps) * here + begin


def tile_plain(rows, tile, energies, sums, want, span):
    own_rows, part_rows = rows
    own_tile, part_tile = tile
    energy_own, energy_part, virt_rows, virt_column = energies
    occ, here = energy_own.shape[0], virt_rows.shape[1]
    there = own_tile.shape[0] // occ
    virt_rows = virt_rows[0]
    virt_tile = lax.dynamic_slice_in_dim(virt_column[:, 0], first_row(span, here), there, 0)
    shape = (occ, there, occ, here)
    diag = contract(own_tile, own_rows).reshape(shape)
    first = contract(part_tile, own_rows).reshape(shape)
    second = contract(own_tile, part_rows).reshape(shape)
    virt = virt_tile[None, :, None, None] + virt_rows[None, None, None, :]
    denom_diag = energy_own[:, None, None, None] + energy_own[None, None, :, None] - virt
    denom_cross = energy_part[:, None, None, None] + energy_own[None, None, :, None] - virt
    swap = (2, 1, 0, 3)
    t_diag = ((2.0 * diag - diag.transpose(swap)) / denom_diag).astype(jnp.bfloat16)
    t_cross = ((2.0 * first - second.transpose(swap)) / denom_cross).astype(jnp.bfloat16)
    t_back = ((2.0 * second - first.transpose(swap)) / denom_cross.transpose(swap)).astype(jnp.bfloat16)

    def spread(amplitudes, rows):
        return lax.dot_general(
            amplitudes.reshape(occ * there, occ * here),
            rows,
            (((0,), (0,)), ((), ())),
            preferred_element_type=jnp.float32,
        )

    terms = {
        "own": lambda: spread(t_diag, own_tile) + spread(t_cross, part_tile),
        "partner": lambda: spread(t_back, own_tile),
    }
    return [terms[name]() if total is None else total + terms[name]() for name, total in zip(want, sums)]


def tile_kernel(
    occ, here, sizes, choices, columns, want, summed, span, energy_own, energy_part, virt_rows, virt_column,
    after, own_rows, part_rows, *refs,
):
    del after
    refs = list(refs)
    own_pieces, part_pieces = [[[refs.pop(0) for _ in range(n)] for n in side] for side in choices]
    sums = refs[:len(want)] if summed else (None,) * len(want)
    refs = refs[len(want):] if summed else refs
    outs = refs[:len(want)]
    done, tiles, gram, first, second, left, sem = refs[len(want):]
    done[...] = jnp.zeros_like(done)
    there = sum(sizes)
    wide = occ * there
    own, partner = "own" in want, "partner" in want
    groups = []
    for which, pieces in enumerate((own_pieces, part_pieces)):
        group, offset = [], 0
        for n, (piece, size) in enumerate(zip(pieces, sizes)):
            for j in range(occ):
                group.append([
                    pltpu.make_async_copy(
                        choice.at[pl.ds(j * size, size)],
                        tiles.at[pl.ds(which * wide + j * there + offset, size)],
                        sem.at[(which * len(sizes) + n) * occ + j],
                    )
                    for choice in piece
                ])
            offset += size
        groups.append(group)
    for copies in groups[0] + groups[1]:
        if len(copies) == 1:
            copies[0].start()
        else:
            pl.when(in_odd_group())(copies[1].start)
            pl.when(jnp.logical_not(in_odd_group()))(copies[0].start)
    for copies in groups[0]:
        copies[0].wait()
    if own:
        gram[...] = contract(tiles[:wide], own_rows[...])
    second[...] = contract(tiles[:wide], part_rows[...])
    for copies in groups[1]:
        copies[0].wait()
    first[...] = contract(tiles[wide:], own_rows[...])
    begin = pl.multiple_of(first_row(span, here), 16)
    virt = virt_column[pl.ds(begin, there)] + virt_rows[...]

    def block(ref, r, c):
        return ref[r * there:(r + 1) * there, c * here:(c + 1) * here]

    def place(column, blocks, c):
        left[c * here:(c + 1) * here, column:column + wide] = (
            jnp.concatenate(blocks, axis=0).T.astype(jnp.bfloat16)
        )

    for i in range(occ):
        if own:
            place(0, [
                (2.0 * block(gram, j, i) - block(gram, i, j)) / (energy_own[i] + energy_own[j] - virt)
                for j in range(occ)
            ], i)
            place(wide, [
                (2.0 * block(first, j, i) - block(second, i, j)) / (energy_own[i] + energy_part[j] - virt)
                for j in range(occ)
            ], i)
    if partner:
        for j in range(occ):
            place(2 * wide if own else 0, [
                (2.0 * block(second, i, j) - block(first, j, i)) / (energy_own[i] + energy_part[j] - virt)
                for i in range(occ)
            ], j)

    for begin in range(0, tiles.shape[1], columns):
        at = slice(begin, begin + columns)
        for name, total, out in zip(want, sums, outs):
            if name == "own":
                term = jnp.dot(left[:, :2 * wide], tiles[:, at], preferred_element_type=jnp.float32)
            else:
                skip = 2 * wide if own else 0
                term = jnp.dot(
                    left[:, skip:skip + wide], tiles[:wide, at], preferred_element_type=jnp.float32
                )
            out[:, at] = (term if total is None else total[:, at] + term).astype(out.dtype)


def tile_terms(rows, pieces, energies, sums, want, span, after, kinds=None):
    energy_own, virt_rows = energies[0], energies[2]
    occ, here = energy_own.shape[0], virt_rows.shape[1]
    aux = rows[0].shape[1]
    pieces = [[p if isinstance(p, tuple) else (p,) for p in side] for side in pieces]
    choices = [[len(p) for p in side] for side in pieces]
    sizes = tuple(p[0].shape[0] // occ for p in pieces[0])
    there = sum(sizes)
    kinds = kinds or (jnp.float32,) * len(want)
    if here % LANES or (occ * there) % LANES or any(size % 16 for size in sizes):
        chosen = [[p[0] if len(p) == 1 else jnp.where(in_odd_group(), p[1], p[0]) for p in side] for side in pieces]
        tile = [
            jnp.concatenate([p.reshape(occ, -1, aux) for p in side], axis=1).reshape(occ * there, aux)
            for side in chosen
        ]
        sums = [t.astype(k) for t, k in zip(tile_plain(rows, tile, energies, sums, want, span), kinds)]
        return *sums, sums[0][:1, :1]
    flat_pieces = [p for side in pieces for choice in side for p in choice]
    columns = min(aux, 512)
    wide, tall = occ * there, occ * here
    summed = sums[0] is not None
    scalar = pl.BlockSpec(memory_space=pltpu.SMEM)
    vmem = pl.BlockSpec(memory_space=pltpu.VMEM)
    hbm = pl.BlockSpec(memory_space=pl.ANY)
    products = 3 if "own" in want else 2
    spreads = (2 if "own" in want else 0) + (1 if "partner" in want else 0)
    return pl.pallas_call(
        functools.partial(tile_kernel, occ, here, sizes, choices, columns, want, summed, span),
        in_specs=[scalar, scalar, vmem, vmem, hbm, vmem, vmem] + [hbm] * len(flat_pieces) + [vmem] * (len(want) * summed),
        out_specs=[vmem] * (len(want) + 1),
        out_shape=[
            pltpu.VMEM((tall, aux), kind) if kind == jnp.float32 else jax.ShapeDtypeStruct((tall, aux), kind)
            for kind in kinds
        ] + [jax.ShapeDtypeStruct((8, LANES), jnp.float32)],
        input_output_aliases={
            7 + len(flat_pieces) + n: n for n, kind in enumerate(kinds) if summed and kind == jnp.float32
        },
        scratch_shapes=[
            pltpu.VMEM((2 * wide, aux), jnp.bfloat16),
            pltpu.VMEM((wide, tall), jnp.float32),
            pltpu.VMEM((wide, tall), jnp.float32),
            pltpu.VMEM((wide, tall), jnp.float32),
            pltpu.VMEM((tall, spreads * wide), jnp.bfloat16),
            pltpu.SemaphoreType.DMA((2 * len(sizes) * occ,)),
        ],
        compiler_params=pltpu.CompilerParams(vmem_limit_bytes=VMEM_BYTES),
        cost_estimate=pl.CostEstimate(flops=0, bytes_accessed=0, transcendentals=0),
    )(
        *energies, after, *rows, *flat_pieces, *(sums if summed else ()),
    )


def local(three_index, occ_energy, virt_energy):
    occ, here, aux = three_index.shape
    steps = lax.axis_size("virt")
    me = lax.axis_index("virt")
    sizes = (here // 2,) * 2 if here % LANES == 0 else (here,)
    offsets = [sum(sizes[:c]) for c in range(len(sizes))]
    cut = len(sizes) // 2
    energy_part = shifted(occ_energy, "blk", 1)
    virt_rows = lax.dynamic_slice_in_dim(virt_energy, me * here, here, 0)
    own_rows = three_index.reshape(occ * here, aux)
    part_rows = shifted(own_rows, "blk", 1)
    rows = (own_rows, part_rows)
    both = ("own", "partner")

    energies = (occ_energy, energy_part, virt_rows[None, :], virt_energy[:, None])
    done = jnp.zeros((1, 1), jnp.float32)

    def terms(step, pieces, sums, want, begin, after, kinds=None):
        after, _ = lax.optimization_barrier((done, after))
        *sums, end = tile_terms(rows, pieces, energies, sums, want, (step, begin), after, kinds)
        return sums, end

    tiles = lax.optimization_barrier([
        three_index[:, o:o + size].reshape(occ * size, aux) for o, size in zip(offsets, sizes)
    ])
    ordered = lax.axis_size("blk") % 2 == 0 and cut > 0 and steps > 2
    moving = [shifted(tile, "virt", 1) for tile in tiles]
    waiting = ([own_rows], [part_rows])
    sums = (None, None)
    for step in range(1, steps - ordered):
        tiles, later, parts = [], [], []
        for c, tile in enumerate(moving):
            tile, *_ = lax.optimization_barrier((tile, done, *(parts or waiting[1])[-1:]))
            tiles.append(tile)
            if step < steps - 1 - ordered:
                later.append(shifted(tile, "virt", 1))
            elif ordered:
                later.append(around(tile, 1))
            parts.append(shifted(tile, "blk", 1))
            if c == 0:
                sums, done = terms(step - 1, waiting, sums, both, 0, tile)
        waiting, moving = (tiles, parts), later
    step = steps - 1
    if ordered:
        crossed, behind = [], []
        for c, tile in enumerate(moving):
            tile, *_ = lax.optimization_barrier((tile, done, (crossed or parts)[-1]))
            moving[c] = tile
            crossed.append(passed(tile, 1, 1))
            if c == 0:
                sums, done = terms(step - 1, waiting, sums, both, 0, tile)
            held = tiles[c]
            if c:
                held, _ = lax.optimization_barrier((held, crossed[c - 1]))
            behind.append(around(held, 0))
        tiles, parts = [], []
        for c, tile in enumerate(behind):
            tile, _ = lax.optimization_barrier((tile, done))
            tiles.append((tile, moving[c]))
            parts.append((crossed[c], passed(tile, 0, 1)))
            if c + 1 == cut:
                sums, done = terms(step, (tiles[:cut], parts[:cut]), sums, both, 0, tile)
    begin = offsets[cut]
    tail = (tiles[cut:], parts[cut:])
    (partner,), done = terms(step, tail, sums[1:], ("partner",), begin, done, (jnp.bfloat16,))
    back = shifted(partner, "blk", -1)
    (own,), done = terms(step, tail, sums[:1], ("own",), begin, done)
    return (own + back.astype(jnp.float32)).astype(jnp.bfloat16).reshape(occ, here, aux)


def solution(mesh):
    placed = (P(("copies", "blk"), "virt", None), P(("copies", "blk")), P("copies"))
    return jax.shard_map(
        local,
        mesh=mesh,
        in_specs=placed,
        out_specs=P(("copies", "blk"), "virt", None),
        check_vma=False,
    )
```

```python
import functools

import jax
import jax.numpy as jnp
from jax import lax
from jax.experimental import pallas as pl
from jax.experimental.pallas import tpu as pltpu
from jax.sharding import PartitionSpec as P

LANES = 128
VMEM_BYTES = 32 * 2**20


def shifted(shard, axis, by):
    devices = lax.axis_size(axis)
    return lax.ppermute(shard, axis, [(i, (i + by) % devices) for i in range(devices)])


def around(shard, odd):
    groups, devices = lax.axis_size("blk"), lax.axis_size("virt")
    return lax.ppermute(shard, ("blk", "virt"), [
        (g * devices + i, g * devices + (i + 1) % devices)
        for g in range(odd, groups, 2)
        for i in range(devices)
    ])


def passed(shard, odd, by):
    groups = lax.axis_size("blk")
    return lax.ppermute(shard, "blk", [(g, (g + by) % groups) for g in range(odd, groups, 2)])


def in_odd_group():
    return lax.rem(lax.axis_index("blk"), 2) == 1


def contract(left, right):
    return lax.dot_general(
        left, right, (((1,), (1,)), ((), ())), preferred_element_type=jnp.float32
    )


def first_row(span, here):
    step, begin = span
    steps = lax.axis_size("virt")
    return lax.rem(lax.axis_index("virt") + (steps - step), steps) * here + begin


def tile_plain(rows, tile, energies, sums, want, spans):
    own_rows, part_rows = rows
    own_tile, part_tile = tile
    energy_own, energy_part, virt_rows, virt_column = energies
    occ, here = energy_own.shape[0], virt_rows.shape[1]
    there = own_tile.shape[0] // occ
    virt_rows = virt_rows[0]
    virt_tile = jnp.concatenate([
        lax.dynamic_slice_in_dim(virt_column[:, 0], first_row(span, here), size, 0) for span, size in spans
    ])
    shape = (occ, there, occ, here)
    diag = contract(own_tile, own_rows).reshape(shape)
    first = contract(part_tile, own_rows).reshape(shape)
    second = contract(own_tile, part_rows).reshape(shape)
    virt = virt_tile[None, :, None, None] + virt_rows[None, None, None, :]
    denom_diag = energy_own[:, None, None, None] + energy_own[None, None, :, None] - virt
    denom_cross = energy_part[:, None, None, None] + energy_own[None, None, :, None] - virt
    swap = (2, 1, 0, 3)
    t_diag = ((2.0 * diag - diag.transpose(swap)) / denom_diag).astype(jnp.bfloat16)
    t_cross = ((2.0 * first - second.transpose(swap)) / denom_cross).astype(jnp.bfloat16)
    t_back = ((2.0 * second - first.transpose(swap)) / denom_cross.transpose(swap)).astype(jnp.bfloat16)

    def spread(amplitudes, rows):
        return lax.dot_general(
            amplitudes.reshape(occ * there, occ * here),
            rows,
            (((0,), (0,)), ((), ())),
            preferred_element_type=jnp.float32,
        )

    terms = {
        "own": lambda: spread(t_diag, own_tile) + spread(t_cross, part_tile),
        "partner": lambda: spread(t_back, own_tile),
    }
    return [terms[name]() if total is None else total + terms[name]() for name, total in zip(want, sums)]


def tile_kernel(
    occ, here, sizes, choices, windows, want, summed, spans, energy_own, energy_part, virt_rows, virt_column,
    after, own_rows, part_rows, *refs,
):
    del after
    refs = list(refs)
    own_pieces, part_pieces = [[[refs.pop(0) for _ in range(n)] for n in side] for side in choices]
    sums = refs[:len(want)] if summed else (None,) * len(want)
    refs = refs[len(want):] if summed else refs
    outs = refs[:len(want)]
    done, tiles, gram, first, second, left, sem = refs[len(want):]
    done[...] = jnp.zeros_like(done)
    there = sum(sizes)
    wide = occ * there
    own, partner = "own" in want, "partner" in want
    groups = []
    for which, pieces in enumerate((own_pieces, part_pieces)):
        group, offset = [], 0
        for n, (piece, size) in enumerate(zip(pieces, sizes)):
            for j in range(occ):
                group.append([
                    pltpu.make_async_copy(
                        choice.at[pl.ds(j * size, size)],
                        tiles.at[pl.ds(which * wide + j * there + offset, size)],
                        sem.at[(which * len(sizes) + n) * occ + j],
                    )
                    for choice in piece
                ])
            offset += size
        groups.append(group)
    for copies in groups[0] + groups[1]:
        if len(copies) == 1:
            copies[0].start()
        else:
            pl.when(in_odd_group())(copies[1].start)
            pl.when(jnp.logical_not(in_odd_group()))(copies[0].start)
    for copies in groups[0]:
        copies[0].wait()
    if own:
        gram[...] = contract(tiles[:wide], own_rows[...])
    second[...] = contract(tiles[:wide], part_rows[...])
    for copies in groups[1]:
        copies[0].wait()
    first[...] = contract(tiles[wide:], own_rows[...])
    virt = jnp.concatenate([
        virt_column[pl.ds(pl.multiple_of(first_row(span, here), 16), size)] for span, size in zip(spans, sizes)
    ]) + virt_rows[...]

    def block(ref, r, c):
        return ref[r * there:(r + 1) * there, c * here:(c + 1) * here]

    def place(column, blocks, c):
        left[c * here:(c + 1) * here, column:column + wide] = (
            jnp.concatenate(blocks, axis=0).T.astype(jnp.bfloat16)
        )

    for i in range(occ):
        if own:
            place(0, [
                (2.0 * block(gram, j, i) - block(gram, i, j)) / (energy_own[i] + energy_own[j] - virt)
                for j in range(occ)
            ], i)
            place(wide, [
                (2.0 * block(first, j, i) - block(second, i, j)) / (energy_own[i] + energy_part[j] - virt)
                for j in range(occ)
            ], i)
    if partner:
        for j in range(occ):
            place(2 * wide if own else 0, [
                (2.0 * block(second, i, j) - block(first, j, i)) / (energy_own[i] + energy_part[j] - virt)
                for i in range(occ)
            ], j)

    for name, total, out, window in zip(want, sums, outs, windows):
        columns = min(window[1] - window[0], 512)
        for begin in range(*window, columns):
            at = slice(begin, begin + columns)
            if name == "own":
                term = jnp.dot(left[:, :2 * wide], tiles[:, at], preferred_element_type=jnp.float32)
            else:
                skip = 2 * wide if own else 0
                term = jnp.dot(
                    left[:, skip:skip + wide], tiles[:wide, at], preferred_element_type=jnp.float32
                )
            term = term if total is None else total[:, at] + term
            out[:, begin - window[0]:begin - window[0] + columns] = term.astype(out.dtype)


def tile_terms(rows, pieces, energies, sums, want, spans, after, kinds=None, windows=None):
    energy_own, virt_rows = energies[0], energies[2]
    occ, here = energy_own.shape[0], virt_rows.shape[1]
    aux = rows[0].shape[1]
    pieces = [[p if isinstance(p, tuple) else (p,) for p in side] for side in pieces]
    choices = [[len(p) for p in side] for side in pieces]
    sizes = tuple(p[0].shape[0] // occ for p in pieces[0])
    there = sum(sizes)
    kinds = kinds or (jnp.float32,) * len(want)
    if here % LANES or (occ * there) % LANES or any(size % 16 for size in sizes):
        chosen = [[p[0] if len(p) == 1 else jnp.where(in_odd_group(), p[1], p[0]) for p in side] for side in pieces]
        tile = [
            jnp.concatenate([p.reshape(occ, -1, aux) for p in side], axis=1).reshape(occ * there, aux)
            for side in chosen
        ]
        terms = tile_plain(rows, tile, energies, sums, want, list(zip(spans, sizes)))
        windows = windows or ((0, aux),) * len(want)
        sums = [t[:, slice(*window)].astype(k) for t, k, window in zip(terms, kinds, windows)]
        return *sums, sums[0][:1, :1]
    flat_pieces = [p for side in pieces for choice in side for p in choice]
    windows = windows or ((0, aux),) * len(want)
    wide, tall = occ * there, occ * here
    summed = sums[0] is not None
    scalar = pl.BlockSpec(memory_space=pltpu.SMEM)
    vmem = pl.BlockSpec(memory_space=pltpu.VMEM)
    hbm = pl.BlockSpec(memory_space=pl.ANY)
    products = 3 if "own" in want else 2
    spreads = (2 if "own" in want else 0) + (1 if "partner" in want else 0)
    return pl.pallas_call(
        functools.partial(tile_kernel, occ, here, sizes, choices, windows, want, summed, spans),
        in_specs=[scalar, scalar, vmem, vmem, hbm, vmem, vmem] + [hbm] * len(flat_pieces) + [vmem] * (len(want) * summed),
        out_specs=[vmem] * (len(want) + 1),
        out_shape=[
            pltpu.VMEM((tall, aux), kind) if kind == jnp.float32
            else jax.ShapeDtypeStruct((tall, window[1] - window[0]), kind)
            for kind, window in zip(kinds, windows)
        ] + [jax.ShapeDtypeStruct((8, LANES), jnp.float32)],
        input_output_aliases={
            7 + len(flat_pieces) + n: n for n, kind in enumerate(kinds) if summed and kind == jnp.float32
        },
        scratch_shapes=[
            pltpu.VMEM((2 * wide, aux), jnp.bfloat16),
            pltpu.VMEM((wide, tall), jnp.float32),
            pltpu.VMEM((wide, tall), jnp.float32),
            pltpu.VMEM((wide, tall), jnp.float32),
            pltpu.VMEM((tall, spreads * wide), jnp.bfloat16),
            pltpu.SemaphoreType.DMA((2 * len(sizes) * occ,)),
        ],
        compiler_params=pltpu.CompilerParams(vmem_limit_bytes=VMEM_BYTES),
        cost_estimate=pl.CostEstimate(flops=0, bytes_accessed=0, transcendentals=0),
    )(
        *energies, after, *rows, *flat_pieces, *(sums if summed else ()),
    )


def finish_kernel(window, begins, own, *refs):
    backs, (out, scratch, sem) = refs[:len(begins)], refs[-3:]
    tall, width = scratch.shape
    strip = tall // sem.shape[0]
    copies = []
    for n in range(sem.shape[0]):
        at = slice(n * strip, (n + 1) * strip)
        total = own[at, window[0]:window[1]]
        for back, begin in zip(backs, begins):
            start = window[0] - begin
            total = total + back[at, start:start + width].astype(jnp.float32)
        scratch[at] = total.astype(scratch.dtype)
        copies.append(pltpu.make_async_copy(scratch.at[at], out.at[at, pl.ds(window[0], width)], sem.at[n]))
        copies[-1].start()
    for copy in copies:
        copy.wait()


def finished(own, backs, windows):
    tall, aux = own.shape
    if tall % LANES:
        return sum((back.astype(jnp.float32) for back, _ in backs), start=own).astype(jnp.bfloat16)
    out = None
    vmem, hbm = pl.BlockSpec(memory_space=pltpu.VMEM), pl.BlockSpec(memory_space=pl.ANY)
    for window in windows:
        near = [(back, span[0]) for back, span in backs if span[0] <= window[0] and window[1] <= span[1]]
        done = [] if out is None else [out]
        out = pl.pallas_call(
            functools.partial(finish_kernel, window, [begin for _, begin in near]),
            in_specs=[vmem] * (1 + len(near)) + [hbm] * len(done),
            out_specs=hbm,
            out_shape=jax.ShapeDtypeStruct((tall, aux), jnp.bfloat16),
            input_output_aliases={1 + len(near): 0} if done else {},
            scratch_shapes=[
                pltpu.VMEM((tall, window[1] - window[0]), jnp.bfloat16),
                pltpu.SemaphoreType.DMA((4,)),
            ],
            compiler_params=pltpu.CompilerParams(vmem_limit_bytes=VMEM_BYTES),
            cost_estimate=pl.CostEstimate(flops=0, bytes_accessed=0, transcendentals=0),
        )(own, *(back for back, _ in near), *done)
    return out


def local(three_index, occ_energy, virt_energy):
    occ, here, aux = three_index.shape
    steps = lax.axis_size("virt")
    me = lax.axis_index("virt")
    sizes = (here // 2,) * 2 if here % LANES == 0 else (here,)
    offsets = [sum(sizes[:c]) for c in range(len(sizes))]
    energy_part = shifted(occ_energy, "blk", 1)
    virt_rows = lax.dynamic_slice_in_dim(virt_energy, me * here, here, 0)
    own_rows = three_index.reshape(occ * here, aux)
    part_rows = shifted(own_rows, "blk", 1)
    rows = (own_rows, part_rows)
    both = ("own", "partner")

    energies = (occ_energy, energy_part, virt_rows[None, :], virt_energy[:, None])
    done = jnp.zeros((1, 1), jnp.float32)

    def terms(runs, pieces, sums, want, after, kinds=None, windows=None):
        after, _ = lax.optimization_barrier((done, after))
        spans = [(step, offsets[c]) for step, c in runs]
        *sums, end = tile_terms(rows, pieces, energies, sums, want, spans, after, kinds, windows)
        return sums, end

    tiles = lax.optimization_barrier([
        three_index[:, o:o + size].reshape(occ * size, aux) for o, size in zip(offsets, sizes)
    ])
    ordered = lax.axis_size("blk") % 2 == 0 and len(sizes) == 2 and steps > 2
    moving = [shifted(tile, "virt", 1) for tile in tiles]
    count = len(sizes)
    waiting, runs = ([own_rows], [part_rows]), [(0, 0)]
    sums = (None, None)
    for step in range(1, steps - ordered):
        tiles, later, parts = [], [], []
        for c, tile in enumerate(moving):
            tile, *_ = lax.optimization_barrier((tile, done, *(parts or waiting[1])[-1:]))
            tiles.append(tile)
            if step < steps - 1 - ordered:
                later.append(shifted(tile, "virt", 1))
            elif ordered:
                later.append(around(tile, 1))
            parts.append(shifted(tile, "blk", 1))
            if c == 0:
                sums, done = terms(runs, waiting, sums, both, tile)
            elif ordered and step == steps - 2:
                sums, done = terms([(step, 0)], (tiles[:1], parts[:1]), sums, both, tile)
        waiting, moving, runs = (tiles, parts), later, [(step, c) for c in range(count)]
    step = steps - 1
    if ordered:
        first, second = moving
        first, *_ = lax.optimization_barrier((first, done, parts[1]))
        crossed = [passed(first, 1, 1)]
        behind = [around(tiles[0], 0)]
        second, held, _ = lax.optimization_barrier((second, tiles[1], crossed[0]))
        crossed.append(passed(second, 1, 1))
        behind.append(around(held, 0))
        beside = [passed(behind[0], 0, 1)]
        early = ([tiles[1], (behind[0], first)], [parts[1], (crossed[0], beside[0])])
        sums, done = terms([(step - 1, 1), (step, 0)], early, sums, both, second)
        windows, runs = ((0, aux),), [(step, 1)]
        chosen = ([behind[1]], [crossed[1]])
        (partner,), done = terms(runs, chosen, sums[1:], ("partner",), done, (jnp.bfloat16,))
        backs = [(passed(partner, 0, -1), windows[0])]
        late, _ = lax.optimization_barrier((behind[1], done))
        beside.append(passed(late, 0, 1))
        tail = ([(late, second)], [(crossed[1], beside[1])])
        chosen = ([second], [beside[1]])
        (partner,), done = terms(runs, chosen, sums[1:], ("partner",), done, (jnp.bfloat16,))
        backs.append((passed(partner, 1, -1), windows[0]))
    else:
        windows, tail = [(0, aux)], waiting
        (partner,), done = terms(runs, tail, sums[1:], ("partner",), done, (jnp.bfloat16,))
        backs = [(shifted(partner, "blk", -1), windows[0])]
    (own,), done = terms(runs, tail, sums[:1], ("own",), done)
    return finished(own, backs, windows).reshape(occ, here, aux)


def solution(mesh):
    placed = (P(("copies", "blk"), "virt", None), P(("copies", "blk")), P("copies"))
    return jax.shard_map(
        local,
        mesh=mesh,
        in_specs=placed,
        out_specs=P(("copies", "blk"), "virt", None),
        check_vma=False,
    )
```

```python
import functools

import jax
import jax.numpy as jnp
from jax import lax
from jax.experimental import pallas as pl
from jax.experimental.pallas import tpu as pltpu
from jax.sharding import PartitionSpec as P

LANES = 128
VMEM_BYTES = 24 * 2**20


def shifted(shard, axis, by):
    devices = lax.axis_size(axis)
    return lax.ppermute(shard, axis, [(i, (i + by) % devices) for i in range(devices)])


def around(shard, odd):
    groups, devices = lax.axis_size("blk"), lax.axis_size("virt")
    return lax.ppermute(shard, ("blk", "virt"), [
        (g * devices + i, g * devices + (i + 1) % devices)
        for g in range(odd, groups, 2)
        for i in range(devices)
    ])


def passed(shard, odd, by):
    groups = lax.axis_size("blk")
    return lax.ppermute(shard, "blk", [(g, (g + by) % groups) for g in range(odd, groups, 2)])


def in_odd_group():
    return lax.rem(lax.axis_index("blk"), 2) == 1


def contract(left, right):
    return lax.dot_general(
        left, right, (((1,), (1,)), ((), ())), preferred_element_type=jnp.float32
    )


def first_row(span, here):
    step, begin = span
    steps = lax.axis_size("virt")
    return lax.rem(lax.axis_index("virt") + (steps - step), steps) * here + begin


def tile_plain(rows, tile, energies, sums, want, spans):
    own_rows, part_rows = rows
    own_tile, part_tile = tile
    energy_own, energy_part, virt_rows, virt_column = energies
    occ, here = energy_own.shape[0], virt_rows.shape[1]
    there = own_tile.shape[0] // occ
    virt_rows = virt_rows[0]
    virt_tile = jnp.concatenate([
        lax.dynamic_slice_in_dim(virt_column[:, 0], first_row(span, here), size, 0) for span, size in spans
    ])
    shape = (occ, there, occ, here)
    diag = contract(own_tile, own_rows).reshape(shape)
    first = contract(part_tile, own_rows).reshape(shape)
    second = contract(own_tile, part_rows).reshape(shape)
    virt = virt_tile[None, :, None, None] + virt_rows[None, None, None, :]
    denom_diag = energy_own[:, None, None, None] + energy_own[None, None, :, None] - virt
    denom_cross = energy_part[:, None, None, None] + energy_own[None, None, :, None] - virt
    swap = (2, 1, 0, 3)
    t_diag = ((2.0 * diag - diag.transpose(swap)) / denom_diag).astype(jnp.bfloat16)
    t_cross = ((2.0 * first - second.transpose(swap)) / denom_cross).astype(jnp.bfloat16)
    t_back = ((2.0 * second - first.transpose(swap)) / denom_cross.transpose(swap)).astype(jnp.bfloat16)

    def spread(amplitudes, rows):
        return lax.dot_general(
            amplitudes.reshape(occ * there, occ * here),
            rows,
            (((0,), (0,)), ((), ())),
            preferred_element_type=jnp.float32,
        )

    terms = {
        "own": lambda: spread(t_diag, own_tile) + spread(t_cross, part_tile),
        "partner": lambda: spread(t_back, own_tile),
    }
    return [terms[name]() if total is None else total + terms[name]() for name, total in zip(want, sums)]


def tile_kernel(
    occ, here, sizes, choices, windows, want, summed, spans, energy_own, energy_part, virt_rows, virt_column,
    after, own_rows, part_rows, *refs,
):
    del after
    refs = list(refs)
    own_pieces, part_pieces = [[[refs.pop(0) for _ in range(n)] for n in side] for side in choices]
    sums = refs[:len(want)] if summed else (None,) * len(want)
    refs = refs[len(want):] if summed else refs
    outs = refs[:len(want)]
    done, tiles, gram, first, second, left, sem = refs[len(want):]
    done[...] = jnp.zeros_like(done)
    there = sum(sizes)
    wide = occ * there
    own, partner = "own" in want, "partner" in want
    groups = []
    for which, pieces in enumerate((own_pieces, part_pieces)):
        group, offset = [], 0
        for n, (piece, size) in enumerate(zip(pieces, sizes)):
            for j in range(occ):
                group.append([
                    pltpu.make_async_copy(
                        choice.at[pl.ds(j * size, size)],
                        tiles.at[pl.ds(which * wide + j * there + offset, size)],
                        sem.at[(which * len(sizes) + n) * occ + j],
                    )
                    for choice in piece
                ])
            offset += size
        groups.append(group)
    for copies in groups[0] + groups[1]:
        if len(copies) == 1:
            copies[0].start()
        else:
            pl.when(in_odd_group())(copies[1].start)
            pl.when(jnp.logical_not(in_odd_group()))(copies[0].start)
    for copies in groups[0]:
        copies[0].wait()
    if own:
        gram[...] = contract(tiles[:wide], own_rows[...])
    second[...] = contract(tiles[:wide], part_rows[...])
    for copies in groups[1]:
        copies[0].wait()
    first[...] = contract(tiles[wide:], own_rows[...])
    virt = jnp.concatenate([
        virt_column[pl.ds(pl.multiple_of(first_row(span, here), 16), size)] for span, size in zip(spans, sizes)
    ]) + virt_rows[...]

    def block(ref, r, c):
        return ref[r * there:(r + 1) * there, c * here:(c + 1) * here]

    def place(column, blocks, c):
        left[c * here:(c + 1) * here, column:column + wide] = (
            jnp.concatenate(blocks, axis=0).T.astype(jnp.bfloat16)
        )

    for i in range(occ):
        if own:
            place(0, [
                (2.0 * block(gram, j, i) - block(gram, i, j)) / (energy_own[i] + energy_own[j] - virt)
                for j in range(occ)
            ], i)
            place(wide, [
                (2.0 * block(first, j, i) - block(second, i, j)) / (energy_own[i] + energy_part[j] - virt)
                for j in range(occ)
            ], i)
    if partner:
        for j in range(occ):
            place(2 * wide if own else 0, [
                (2.0 * block(second, i, j) - block(first, j, i)) / (energy_own[i] + energy_part[j] - virt)
                for i in range(occ)
            ], j)

    for name, total, out, window in zip(want, sums, outs, windows):
        columns = min(window[1] - window[0], 512)
        for begin in range(*window, columns):
            at = slice(begin, begin + columns)
            if name == "own":
                term = jnp.dot(left[:, :2 * wide], tiles[:, at], preferred_element_type=jnp.float32)
            else:
                skip = 2 * wide if own else 0
                term = jnp.dot(
                    left[:, skip:skip + wide], tiles[:wide, at], preferred_element_type=jnp.float32
                )
            term = term if total is None else total[:, at] + term
            out[:, begin - window[0]:begin - window[0] + columns] = term.astype(out.dtype)


def tile_terms(rows, pieces, energies, sums, want, spans, after, kinds=None, windows=None, keep=False):
    energy_own, virt_rows = energies[0], energies[2]
    occ, here = energy_own.shape[0], virt_rows.shape[1]
    aux = rows[0].shape[1]
    pieces = [[p if isinstance(p, tuple) else (p,) for p in side] for side in pieces]
    choices = [[len(p) for p in side] for side in pieces]
    sizes = tuple(p[0].shape[0] // occ for p in pieces[0])
    there = sum(sizes)
    kinds = kinds or (jnp.float32,) * len(want)
    if here % LANES or (occ * there) % LANES or any(size % 16 for size in sizes):
        chosen = [[p[0] if len(p) == 1 else jnp.where(in_odd_group(), p[1], p[0]) for p in side] for side in pieces]
        tile = [
            jnp.concatenate([p.reshape(occ, -1, aux) for p in side], axis=1).reshape(occ * there, aux)
            for side in chosen
        ]
        terms = tile_plain(rows, tile, energies, sums, want, list(zip(spans, sizes)))
        windows = windows or ((0, aux),) * len(want)
        sums = [t[:, slice(*window)].astype(k) for t, k, window in zip(terms, kinds, windows)]
        return *sums, sums[0][:1, :1]
    flat_pieces = [p for side in pieces for choice in side for p in choice]
    windows = windows or ((0, aux),) * len(want)
    wide, tall = occ * there, occ * here
    summed = sums[0] is not None
    scalar = pl.BlockSpec(memory_space=pltpu.SMEM)
    vmem = pl.BlockSpec(memory_space=pltpu.VMEM)
    hbm = pl.BlockSpec(memory_space=pl.ANY)
    products = 3 if "own" in want else 2
    spreads = (2 if "own" in want else 0) + (1 if "partner" in want else 0)
    return pl.pallas_call(
        functools.partial(tile_kernel, occ, here, sizes, choices, windows, want, summed, spans),
        in_specs=[scalar, scalar, vmem, vmem, hbm, vmem, vmem] + [hbm] * len(flat_pieces) + [vmem] * (len(want) * summed),
        out_specs=[vmem] * (len(want) + 1),
        out_shape=[
            pltpu.VMEM((tall, aux), kind) if kind == jnp.float32
            else jax.ShapeDtypeStruct((tall, window[1] - window[0]), kind)
            for kind, window in zip(kinds, windows)
        ] + [jax.ShapeDtypeStruct((8, LANES), jnp.float32)],
        input_output_aliases={
            7 + len(flat_pieces) + n: n for n, kind in enumerate(kinds)
            if summed and kind == jnp.float32 and not keep
        },
        scratch_shapes=[
            pltpu.VMEM((2 * wide, aux), jnp.bfloat16),
            pltpu.VMEM((wide, tall), jnp.float32),
            pltpu.VMEM((wide, tall), jnp.float32),
            pltpu.VMEM((wide, tall), jnp.float32),
            pltpu.VMEM((tall, spreads * wide), jnp.bfloat16),
            pltpu.SemaphoreType.DMA((2 * len(sizes) * occ,)),
        ],
        compiler_params=pltpu.CompilerParams(vmem_limit_bytes=VMEM_BYTES),
        cost_estimate=pl.CostEstimate(flops=0, bytes_accessed=0, transcendentals=0),
    )(
        *energies, after, *rows, *flat_pieces, *(sums if summed else ()),
    )


def finish_kernel(window, begins, own, *refs):
    backs, (out, scratch, sem) = refs[:len(begins)], refs[-3:]
    tall, width = scratch.shape
    strip = tall // sem.shape[0]
    copies = []
    for n in range(sem.shape[0]):
        at = slice(n * strip, (n + 1) * strip)
        total = own[at, window[0]:window[1]]
        for back, begin in zip(backs, begins):
            start = window[0] - begin
            total = total + back[at, start:start + width].astype(jnp.float32)
        scratch[at] = total.astype(scratch.dtype)
        copies.append(pltpu.make_async_copy(scratch.at[at], out.at[at, pl.ds(window[0], width)], sem.at[n]))
        copies[-1].start()
    for copy in copies:
        copy.wait()


def finished(own, backs, windows):
    tall, aux = own.shape
    if tall % LANES:
        return sum((back.astype(jnp.float32) for back, _ in backs), start=own).astype(jnp.bfloat16)
    out = None
    vmem, hbm = pl.BlockSpec(memory_space=pltpu.VMEM), pl.BlockSpec(memory_space=pl.ANY)
    for window in windows:
        near = [(back, span[0]) for back, span in backs if span[0] <= window[0] and window[1] <= span[1]]
        done = [] if out is None else [out]
        out = pl.pallas_call(
            functools.partial(finish_kernel, window, [begin for _, begin in near]),
            in_specs=[vmem] * (1 + len(near)) + [hbm] * len(done),
            out_specs=hbm,
            out_shape=jax.ShapeDtypeStruct((tall, aux), jnp.bfloat16),
            input_output_aliases={1 + len(near): 0} if done else {},
            scratch_shapes=[
                pltpu.VMEM((tall, window[1] - window[0]), jnp.bfloat16),
                pltpu.SemaphoreType.DMA((4,)),
            ],
            compiler_params=pltpu.CompilerParams(vmem_limit_bytes=VMEM_BYTES),
            cost_estimate=pl.CostEstimate(flops=0, bytes_accessed=0, transcendentals=0),
        )(own, *(back for back, _ in near), *done)
    return out


def local(three_index, occ_energy, virt_energy):
    occ, here, aux = three_index.shape
    steps = lax.axis_size("virt")
    me = lax.axis_index("virt")
    sizes = (here // 2,) * 2 if here % LANES == 0 else (here,)
    offsets = [sum(sizes[:c]) for c in range(len(sizes))]
    energy_part = shifted(occ_energy, "blk", 1)
    virt_rows = lax.dynamic_slice_in_dim(virt_energy, me * here, here, 0)
    own_rows = three_index.reshape(occ * here, aux)
    part_rows = shifted(own_rows, "blk", 1)
    rows = (own_rows, part_rows)
    both = ("own", "partner")

    energies = (occ_energy, energy_part, virt_rows[None, :], virt_energy[:, None])
    done = jnp.zeros((1, 1), jnp.float32)

    def terms(runs, pieces, sums, want, after, kinds=None, windows=None, keep=False):
        after, _ = lax.optimization_barrier((done, after))
        spans = [(step, offsets[c]) for step, c in runs]
        *sums, end = tile_terms(rows, pieces, energies, sums, want, spans, after, kinds, windows, keep)
        return sums, end

    tiles = lax.optimization_barrier([
        three_index[:, o:o + size].reshape(occ * size, aux) for o, size in zip(offsets, sizes)
    ])
    ordered = lax.axis_size("blk") % 2 == 0 and len(sizes) == 2 and steps > 2
    moving = [shifted(tile, "virt", 1) for tile in tiles]
    count = len(sizes)
    waiting, runs = ([own_rows], [part_rows]), [(0, 0)]
    sums = (None, None)
    for step in range(1, steps - ordered):
        tiles, later, parts = [], [], []
        for c, tile in enumerate(moving):
            tile, *_ = lax.optimization_barrier((tile, done, *(parts or waiting[1])[-1:]))
            tiles.append(tile)
            if step < steps - 1 - ordered:
                later.append(shifted(tile, "virt", 1))
            elif ordered:
                later.append(around(tile, 1))
            parts.append(shifted(tile, "blk", 1))
            if c == 0:
                sums, done = terms(runs, waiting, sums, both, tile)
            elif ordered and step == steps - 2:
                sums, done = terms([(step, 0)], (tiles[:1], parts[:1]), sums, both, tile)
        waiting, moving, runs = (tiles, parts), later, [(step, c) for c in range(count)]
    step = steps - 1
    if ordered:
        first, second = moving
        first, *_ = lax.optimization_barrier((first, done, parts[1]))
        crossed = [passed(first, 1, 1)]
        sums, done = terms([(step - 1, 1)], (tiles[1:], parts[1:]), sums, both, first)
        held, _ = lax.optimization_barrier((tiles[0], first))
        kept, _ = lax.optimization_barrier((tiles[1], first))
        behind = [around(held, 0), around(kept, 0)]
        second, _ = lax.optimization_barrier((second, crossed[0]))
        crossed.append(passed(second, 1, 1))
        ahead, windows, runs = [first, second], ((0, aux),), [(step, 0), (step, 1)]
        ready, done = terms(runs[:1], (behind[:1], crossed[:1]), sums[1:], ("partner",), done, keep=True)
        (partner,), done = terms(
            runs[1:], (behind[1:], crossed[1:]), ready, ("partner",), done, (jnp.bfloat16,)
        )
        backs = [(passed(partner, 0, -1), windows[0])]
        late, _ = lax.optimization_barrier((behind[1], done))
        beside = [passed(behind[0], 0, 1), passed(late, 0, 1)]
        (partner,), done = terms(runs, (ahead, beside), sums[1:], ("partner",), done, (jnp.bfloat16,))
        backs.append((passed(partner, 1, -1), windows[0]))
        tail = (list(zip(behind, ahead)), list(zip(crossed, beside)))
    else:
        windows, tail = [(0, aux)], waiting
        (partner,), done = terms(runs, tail, sums[1:], ("partner",), done, (jnp.bfloat16,))
        backs = [(shifted(partner, "blk", -1), windows[0])]
    (own,), done = terms(runs, tail, sums[:1], ("own",), done)
    return finished(own, backs, windows).reshape(occ, here, aux)


def solution(mesh):
    placed = (P(("copies", "blk"), "virt", None), P(("copies", "blk")), P("copies"))
    return jax.shard_map(
        local,
        mesh=mesh,
        in_specs=placed,
        out_specs=P(("copies", "blk"), "virt", None),
        check_vma=False,
    )
```

```python
import functools

import jax
import jax.numpy as jnp
from jax import lax
from jax.experimental import pallas as pl
from jax.experimental.pallas import tpu as pltpu
from jax.sharding import PartitionSpec as P

LANES = 128
VMEM_BYTES = 32 * 2**20


def shifted(shard, axis, by):
    devices = lax.axis_size(axis)
    return lax.ppermute(shard, axis, [(i, (i + by) % devices) for i in range(devices)])


def around(shard, odd):
    groups, devices = lax.axis_size("blk"), lax.axis_size("virt")
    return lax.ppermute(shard, ("blk", "virt"), [
        (g * devices + i, g * devices + (i + 1) % devices)
        for g in range(odd, groups, 2)
        for i in range(devices)
    ])


def passed(shard, odd, by):
    groups = lax.axis_size("blk")
    return lax.ppermute(shard, "blk", [(g, (g + by) % groups) for g in range(odd, groups, 2)])


def in_odd_group():
    return lax.rem(lax.axis_index("blk"), 2) == 1


def contract(left, right):
    return lax.dot_general(
        left, right, (((1,), (1,)), ((), ())), preferred_element_type=jnp.float32
    )


def first_row(span, here):
    step, begin = span
    steps = lax.axis_size("virt")
    return lax.rem(lax.axis_index("virt") + (steps - step), steps) * here + begin


def tile_plain(rows, tile, energies, sums, want, spans):
    own_rows, part_rows = rows
    own_tile, part_tile = tile
    energy_own, energy_part, virt_rows, virt_column = energies
    occ, here = energy_own.shape[0], virt_rows.shape[1]
    there = own_tile.shape[0] // occ
    virt_rows = virt_rows[0]
    virt_tile = jnp.concatenate([
        lax.dynamic_slice_in_dim(virt_column[:, 0], first_row(span, here), size, 0) for span, size in spans
    ])
    shape = (occ, there, occ, here)
    diag = contract(own_tile, own_rows).reshape(shape)
    first = contract(part_tile, own_rows).reshape(shape)
    second = contract(own_tile, part_rows).reshape(shape)
    virt = virt_tile[None, :, None, None] + virt_rows[None, None, None, :]
    denom_diag = energy_own[:, None, None, None] + energy_own[None, None, :, None] - virt
    denom_cross = energy_part[:, None, None, None] + energy_own[None, None, :, None] - virt
    swap = (2, 1, 0, 3)
    t_diag = ((2.0 * diag - diag.transpose(swap)) / denom_diag).astype(jnp.bfloat16)
    t_cross = ((2.0 * first - second.transpose(swap)) / denom_cross).astype(jnp.bfloat16)
    t_back = ((2.0 * second - first.transpose(swap)) / denom_cross.transpose(swap)).astype(jnp.bfloat16)

    def spread(amplitudes, rows):
        return lax.dot_general(
            amplitudes.reshape(occ * there, occ * here),
            rows,
            (((0,), (0,)), ((), ())),
            preferred_element_type=jnp.float32,
        )

    terms = {
        "own": lambda: spread(t_diag, own_tile) + spread(t_cross, part_tile),
        "partner": lambda: spread(t_back, own_tile),
    }
    return [terms[name]() if total is None else total + terms[name]() for name, total in zip(want, sums)]


def tile_kernel(
    occ, here, sizes, choices, windows, want, summed, spans, energy_own, energy_part, virt_rows, virt_column,
    after, own_rows, part_rows, *refs,
):
    del after
    refs = list(refs)
    own_pieces, part_pieces = [[[refs.pop(0) for _ in range(n)] for n in side] for side in choices]
    sums = refs[:len(want)] if summed else (None,) * len(want)
    refs = refs[len(want):] if summed else refs
    outs = refs[:len(want)]
    done, tiles, gram, first, second, left, sem = refs[len(want):]
    done[...] = jnp.zeros_like(done)
    there = sum(sizes)
    wide = occ * there
    own, partner = "own" in want, "partner" in want
    groups = []
    for which, pieces in enumerate((own_pieces, part_pieces)):
        group, offset = [], 0
        for n, (piece, size) in enumerate(zip(pieces, sizes)):
            for j in range(occ):
                group.append([
                    pltpu.make_async_copy(
                        choice.at[pl.ds(j * size, size)],
                        tiles.at[pl.ds(which * wide + j * there + offset, size)],
                        sem.at[(which * len(sizes) + n) * occ + j],
                    )
                    for choice in piece
                ])
            offset += size
        groups.append(group)
    for copies in groups[0] + groups[1]:
        if len(copies) == 1:
            copies[0].start()
        else:
            pl.when(in_odd_group())(copies[1].start)
            pl.when(jnp.logical_not(in_odd_group()))(copies[0].start)
    for copies in groups[0]:
        copies[0].wait()
    if own:
        gram[...] = contract(tiles[:wide], own_rows[...])
    second[...] = contract(tiles[:wide], part_rows[...])
    for copies in groups[1]:
        copies[0].wait()
    first[...] = contract(tiles[wide:], own_rows[...])
    virt = jnp.concatenate([
        virt_column[pl.ds(pl.multiple_of(first_row(span, here), 16), size)] for span, size in zip(spans, sizes)
    ]) + virt_rows[...]

    def block(ref, r, c):
        return ref[r * there:(r + 1) * there, c * here:(c + 1) * here]

    def place(column, blocks, c):
        left[c * here:(c + 1) * here, column:column + wide] = (
            jnp.concatenate(blocks, axis=0).T.astype(jnp.bfloat16)
        )

    for i in range(occ):
        if own:
            place(0, [
                (2.0 * block(gram, j, i) - block(gram, i, j)) / (energy_own[i] + energy_own[j] - virt)
                for j in range(occ)
            ], i)
            place(wide, [
                (2.0 * block(first, j, i) - block(second, i, j)) / (energy_own[i] + energy_part[j] - virt)
                for j in range(occ)
            ], i)
    if partner:
        for j in range(occ):
            place(2 * wide if own else 0, [
                (2.0 * block(second, i, j) - block(first, j, i)) / (energy_own[i] + energy_part[j] - virt)
                for i in range(occ)
            ], j)

    for name, total, out, window in zip(want, sums, outs, windows):
        columns = min(window[1] - window[0], 512)
        for begin in range(*window, columns):
            at = slice(begin, begin + columns)
            if name == "own":
                term = jnp.dot(left[:, :2 * wide], tiles[:, at], preferred_element_type=jnp.float32)
            else:
                skip = 2 * wide if own else 0
                term = jnp.dot(
                    left[:, skip:skip + wide], tiles[:wide, at], preferred_element_type=jnp.float32
                )
            term = term if total is None else total[:, at] + term
            out[:, begin - window[0]:begin - window[0] + columns] = term.astype(out.dtype)


def tile_terms(rows, pieces, energies, sums, want, spans, after, kinds=None, windows=None):
    energy_own, virt_rows = energies[0], energies[2]
    occ, here = energy_own.shape[0], virt_rows.shape[1]
    aux = rows[0].shape[1]
    pieces = [[p if isinstance(p, tuple) else (p,) for p in side] for side in pieces]
    choices = [[len(p) for p in side] for side in pieces]
    sizes = tuple(p[0].shape[0] // occ for p in pieces[0])
    there = sum(sizes)
    kinds = kinds or (jnp.float32,) * len(want)
    if here % LANES or (occ * there) % LANES or any(size % 16 for size in sizes):
        chosen = [[p[0] if len(p) == 1 else jnp.where(in_odd_group(), p[1], p[0]) for p in side] for side in pieces]
        tile = [
            jnp.concatenate([p.reshape(occ, -1, aux) for p in side], axis=1).reshape(occ * there, aux)
            for side in chosen
        ]
        terms = tile_plain(rows, tile, energies, sums, want, list(zip(spans, sizes)))
        windows = windows or ((0, aux),) * len(want)
        sums = [t[:, slice(*window)].astype(k) for t, k, window in zip(terms, kinds, windows)]
        return *sums, sums[0][:1, :1]
    flat_pieces = [p for side in pieces for choice in side for p in choice]
    windows = windows or ((0, aux),) * len(want)
    wide, tall = occ * there, occ * here
    summed = sums[0] is not None
    scalar = pl.BlockSpec(memory_space=pltpu.SMEM)
    vmem = pl.BlockSpec(memory_space=pltpu.VMEM)
    hbm = pl.BlockSpec(memory_space=pl.ANY)
    products = 3 if "own" in want else 2
    spreads = (2 if "own" in want else 0) + (1 if "partner" in want else 0)
    return pl.pallas_call(
        functools.partial(tile_kernel, occ, here, sizes, choices, windows, want, summed, spans),
        in_specs=[scalar, scalar, vmem, vmem, hbm, vmem, vmem] + [hbm] * len(flat_pieces) + [vmem] * (len(want) * summed),
        out_specs=[vmem] * (len(want) + 1),
        out_shape=[
            pltpu.VMEM((tall, aux), kind) if kind == jnp.float32
            else jax.ShapeDtypeStruct((tall, window[1] - window[0]), kind)
            for kind, window in zip(kinds, windows)
        ] + [jax.ShapeDtypeStruct((8, LANES), jnp.float32)],
        input_output_aliases={
            7 + len(flat_pieces) + n: n for n, kind in enumerate(kinds) if summed and kind == jnp.float32
        },
        scratch_shapes=[
            pltpu.VMEM((2 * wide, aux), jnp.bfloat16),
            pltpu.VMEM((wide, tall), jnp.float32),
            pltpu.VMEM((wide, tall), jnp.float32),
            pltpu.VMEM((wide, tall), jnp.float32),
            pltpu.VMEM((tall, spreads * wide), jnp.bfloat16),
            pltpu.SemaphoreType.DMA((2 * len(sizes) * occ,)),
        ],
        compiler_params=pltpu.CompilerParams(vmem_limit_bytes=VMEM_BYTES),
        cost_estimate=pl.CostEstimate(flops=0, bytes_accessed=0, transcendentals=0),
    )(
        *energies, after, *rows, *flat_pieces, *(sums if summed else ()),
    )


def finish_kernel(window, begins, own, *refs):
    backs, (out, scratch, sem) = refs[:len(begins)], refs[-3:]
    tall, width = scratch.shape
    strip = tall // sem.shape[0]
    copies = []
    for n in range(sem.shape[0]):
        at = slice(n * strip, (n + 1) * strip)
        total = own[at, window[0]:window[1]]
        for back, begin in zip(backs, begins):
            start = window[0] - begin
            total = total + back[at, start:start + width].astype(jnp.float32)
        scratch[at] = total.astype(scratch.dtype)
        copies.append(pltpu.make_async_copy(scratch.at[at], out.at[at, pl.ds(window[0], width)], sem.at[n]))
        copies[-1].start()
    for copy in copies:
        copy.wait()


def finished(own, backs, windows):
    tall, aux = own.shape
    if tall % LANES:
        return sum((back.astype(jnp.float32) for back, _ in backs), start=own).astype(jnp.bfloat16)
    out = None
    vmem, hbm = pl.BlockSpec(memory_space=pltpu.VMEM), pl.BlockSpec(memory_space=pl.ANY)
    for window in windows:
        near = [(back, span[0]) for back, span in backs if span[0] <= window[0] and window[1] <= span[1]]
        done = [] if out is None else [out]
        out = pl.pallas_call(
            functools.partial(finish_kernel, window, [begin for _, begin in near]),
            in_specs=[vmem] * (1 + len(near)) + [hbm] * len(done),
            out_specs=hbm,
            out_shape=jax.ShapeDtypeStruct((tall, aux), jnp.bfloat16),
            input_output_aliases={1 + len(near): 0} if done else {},
            scratch_shapes=[
                pltpu.VMEM((tall, window[1] - window[0]), jnp.bfloat16),
                pltpu.SemaphoreType.DMA((4,)),
            ],
            compiler_params=pltpu.CompilerParams(vmem_limit_bytes=VMEM_BYTES),
            cost_estimate=pl.CostEstimate(flops=0, bytes_accessed=0, transcendentals=0),
        )(own, *(back for back, _ in near), *done)
    return out


def local(three_index, occ_energy, virt_energy):
    occ, here, aux = three_index.shape
    steps = lax.axis_size("virt")
    me = lax.axis_index("virt")
    sizes = (here // 2,) * 2 if here % LANES == 0 else (here,)
    offsets = [sum(sizes[:c]) for c in range(len(sizes))]
    energy_part = shifted(occ_energy, "blk", 1)
    virt_rows = lax.dynamic_slice_in_dim(virt_energy, me * here, here, 0)
    own_rows = three_index.reshape(occ * here, aux)
    part_rows = shifted(own_rows, "blk", 1)
    rows = (own_rows, part_rows)
    both = ("own", "partner")

    energies = (occ_energy, energy_part, virt_rows[None, :], virt_energy[:, None])
    done = jnp.zeros((1, 1), jnp.float32)

    def terms(runs, pieces, sums, want, after, kinds=None, windows=None):
        after, _ = lax.optimization_barrier((done, after))
        spans = [(step, offsets[c]) for step, c in runs]
        *sums, end = tile_terms(rows, pieces, energies, sums, want, spans, after, kinds, windows)
        return sums, end

    tiles = lax.optimization_barrier([
        three_index[:, o:o + size].reshape(occ * size, aux) for o, size in zip(offsets, sizes)
    ])
    ordered = lax.axis_size("blk") % 2 == 0 and len(sizes) == 2 and steps > 2
    moving = [shifted(tile, "virt", 1) for tile in tiles]
    count = len(sizes)
    waiting, runs = ([own_rows], [part_rows]), [(0, 0)]
    sums = (None, None)
    for step in range(1, steps - ordered):
        tiles, later, parts = [], [], []
        for c, tile in enumerate(moving):
            tile, *_ = lax.optimization_barrier((tile, done, *(parts or waiting[1])[-1:]))
            tiles.append(tile)
            if step < steps - 1 - ordered:
                later.append(shifted(tile, "virt", 1))
            elif ordered:
                later.append(around(tile, 1))
            parts.append(shifted(tile, "blk", 1))
            if c == 0:
                sums, done = terms(runs, waiting, sums, both, tile)
            elif ordered and step == steps - 2:
                sums, done = terms([(step, 0)], (tiles[:1], parts[:1]), sums, both, tile)
        waiting, moving, runs = (tiles, parts), later, [(step, c) for c in range(count)]
    step = steps - 1
    if ordered:
        first, second = moving
        first, *_ = lax.optimization_barrier((first, done, parts[1]))
        crossed = [passed(first, 1, 1)]
        sums, done = terms([(step - 1, 1)], (tiles[1:], parts[1:]), sums, both, first)
        held, _ = lax.optimization_barrier((tiles[0], first))
        kept, _ = lax.optimization_barrier((tiles[1], first))
        behind = [around(held, 0), around(kept, 0)]
        second, _ = lax.optimization_barrier((second, crossed[0]))
        crossed.append(passed(second, 1, 1))
        ahead, windows, runs = [first, second], ((0, aux),), [(step, 0), (step, 1)]
        (partner,), done = terms(runs, (behind, crossed), sums[1:], ("partner",), done, (jnp.bfloat16,))
        backs = [(passed(partner, 0, -1), windows[0])]
        late, _ = lax.optimization_barrier((behind[1], done))
        beside = [passed(behind[0], 0, 1), passed(late, 0, 1)]
        (partner,), done = terms(runs, (ahead, beside), sums[1:], ("partner",), done, (jnp.bfloat16,))
        backs.append((passed(partner, 1, -1), windows[0]))
        tail = (list(zip(behind, ahead)), list(zip(crossed, beside)))
    else:
        windows, tail = [(0, aux)], waiting
        (partner,), done = terms(runs, tail, sums[1:], ("partner",), done, (jnp.bfloat16,))
        backs = [(shifted(partner, "blk", -1), windows[0])]
    (own,), done = terms(runs, tail, sums[:1], ("own",), done)
    return finished(own, backs, windows).reshape(occ, here, aux)


def solution(mesh):
    placed = (P(("copies", "blk"), "virt", None), P(("copies", "blk")), P("copies"))
    return jax.shard_map(
        local,
        mesh=mesh,
        in_specs=placed,
        out_specs=P(("copies", "blk"), "virt", None),
        check_vma=False,
    )
```

```python
import functools

import jax
import jax.numpy as jnp
from jax import lax
from jax.experimental import pallas as pl
from jax.experimental.pallas import tpu as pltpu
from jax.sharding import PartitionSpec as P

LANES = 128
VMEM_BYTES = 24 * 2**20


def shifted(shard, axis, by):
    devices = lax.axis_size(axis)
    return lax.ppermute(shard, axis, [(i, (i + by) % devices) for i in range(devices)])


def around(shard, odd):
    groups, devices = lax.axis_size("blk"), lax.axis_size("virt")
    return lax.ppermute(shard, ("blk", "virt"), [
        (g * devices + i, g * devices + (i + 1) % devices)
        for g in range(odd, groups, 2)
        for i in range(devices)
    ])


def passed(shard, odd, by):
    groups = lax.axis_size("blk")
    return lax.ppermute(shard, "blk", [(g, (g + by) % groups) for g in range(odd, groups, 2)])


def in_odd_group():
    return lax.rem(lax.axis_index("blk"), 2) == 1


def contract(left, right):
    return lax.dot_general(
        left, right, (((1,), (1,)), ((), ())), preferred_element_type=jnp.float32
    )


def first_row(span, here):
    step, begin = span
    steps = lax.axis_size("virt")
    return lax.rem(lax.axis_index("virt") + (steps - step), steps) * here + begin


def tile_plain(rows, tile, energies, sums, want, spans):
    own_rows, part_rows = rows
    own_tile, part_tile = tile
    energy_own, energy_part, virt_rows, virt_column = energies
    occ, here = energy_own.shape[0], virt_rows.shape[1]
    there = own_tile.shape[0] // occ
    virt_rows = virt_rows[0]
    virt_tile = jnp.concatenate([
        lax.dynamic_slice_in_dim(virt_column[:, 0], first_row(span, here), size, 0) for span, size in spans
    ])
    shape = (occ, there, occ, here)
    diag = contract(own_tile, own_rows).reshape(shape)
    first = contract(part_tile, own_rows).reshape(shape)
    second = contract(own_tile, part_rows).reshape(shape)
    virt = virt_tile[None, :, None, None] + virt_rows[None, None, None, :]
    denom_diag = energy_own[:, None, None, None] + energy_own[None, None, :, None] - virt
    denom_cross = energy_part[:, None, None, None] + energy_own[None, None, :, None] - virt
    swap = (2, 1, 0, 3)
    t_diag = ((2.0 * diag - diag.transpose(swap)) / denom_diag).astype(jnp.bfloat16)
    t_cross = ((2.0 * first - second.transpose(swap)) / denom_cross).astype(jnp.bfloat16)
    t_back = ((2.0 * second - first.transpose(swap)) / denom_cross.transpose(swap)).astype(jnp.bfloat16)

    def spread(amplitudes, rows):
        return lax.dot_general(
            amplitudes.reshape(occ * there, occ * here),
            rows,
            (((0,), (0,)), ((), ())),
            preferred_element_type=jnp.float32,
        )

    terms = {
        "own": lambda: spread(t_diag, own_tile) + spread(t_cross, part_tile),
        "partner": lambda: spread(t_back, own_tile),
    }
    return [terms[name]() if total is None else total + terms[name]() for name, total in zip(want, sums)]


def tile_kernel(
    occ, here, sizes, choices, windows, want, summed, spans, energy_own, energy_part, virt_rows, virt_column,
    after, own_rows, part_rows, *refs,
):
    del after
    refs = list(refs)
    own_pieces, part_pieces = [[[refs.pop(0) for _ in range(n)] for n in side] for side in choices]
    sums = refs[:len(want)] if summed else (None,) * len(want)
    refs = refs[len(want):] if summed else refs
    outs = refs[:len(want)]
    done, tiles, gram, first, second, left, sem = refs[len(want):]
    done[...] = jnp.zeros_like(done)
    there = sum(sizes)
    wide = occ * there
    own, partner = "own" in want, "partner" in want
    groups = []
    for which, pieces in enumerate((own_pieces, part_pieces)):
        group, offset = [], 0
        for n, (piece, size) in enumerate(zip(pieces, sizes)):
            for j in range(occ):
                group.append([
                    pltpu.make_async_copy(
                        choice.at[pl.ds(j * size, size)],
                        tiles.at[pl.ds(which * wide + j * there + offset, size)],
                        sem.at[(which * len(sizes) + n) * occ + j],
                    )
                    for choice in piece
                ])
            offset += size
        groups.append(group)
    for copies in groups[0] + groups[1]:
        if len(copies) == 1:
            copies[0].start()
        else:
            pl.when(in_odd_group())(copies[1].start)
            pl.when(jnp.logical_not(in_odd_group()))(copies[0].start)
    for copies in groups[0]:
        copies[0].wait()
    if own:
        gram[...] = contract(tiles[:wide], own_rows[...])
    second[...] = contract(tiles[:wide], part_rows[...])
    for copies in groups[1]:
        copies[0].wait()
    first[...] = contract(tiles[wide:], own_rows[...])
    virt = jnp.concatenate([
        virt_column[pl.ds(pl.multiple_of(first_row(span, here), 16), size)] for span, size in zip(spans, sizes)
    ]) + virt_rows[...]

    def block(ref, r, c):
        return ref[r * there:(r + 1) * there, c * here:(c + 1) * here]

    def place(column, blocks, c):
        left[c * here:(c + 1) * here, column:column + wide] = (
            jnp.concatenate(blocks, axis=0).T.astype(jnp.bfloat16)
        )

    for i in range(occ):
        if own:
            place(0, [
                (2.0 * block(gram, j, i) - block(gram, i, j)) / (energy_own[i] + energy_own[j] - virt)
                for j in range(occ)
            ], i)
            place(wide, [
                (2.0 * block(first, j, i) - block(second, i, j)) / (energy_own[i] + energy_part[j] - virt)
                for j in range(occ)
            ], i)
    if partner:
        for j in range(occ):
            place(2 * wide if own else 0, [
                (2.0 * block(second, i, j) - block(first, j, i)) / (energy_own[i] + energy_part[j] - virt)
                for i in range(occ)
            ], j)

    for name, total, out, window in zip(want, sums, outs, windows):
        columns = min(window[1] - window[0], 512)

        @pl.loop(0, (window[1] - window[0]) // columns)
        def _(n):
            begin = pl.multiple_of(n * columns, columns)
            at = pl.ds(begin + window[0], columns)
            if name == "own":
                term = jnp.dot(left[:, :2 * wide], tiles[:, at], preferred_element_type=jnp.float32)
            else:
                skip = 2 * wide if own else 0
                term = jnp.dot(
                    left[:, skip:skip + wide], tiles[:wide, at], preferred_element_type=jnp.float32
                )
            term = term if total is None else total[:, at] + term
            out[:, pl.ds(begin, columns)] = term.astype(out.dtype)


def tile_terms(rows, pieces, energies, sums, want, spans, after, kinds=None, windows=None, keep=False):
    energy_own, virt_rows = energies[0], energies[2]
    occ, here = energy_own.shape[0], virt_rows.shape[1]
    aux = rows[0].shape[1]
    pieces = [[p if isinstance(p, tuple) else (p,) for p in side] for side in pieces]
    choices = [[len(p) for p in side] for side in pieces]
    sizes = tuple(p[0].shape[0] // occ for p in pieces[0])
    there = sum(sizes)
    kinds = kinds or (jnp.float32,) * len(want)
    if here % LANES or (occ * there) % LANES or any(size % 16 for size in sizes):
        chosen = [[p[0] if len(p) == 1 else jnp.where(in_odd_group(), p[1], p[0]) for p in side] for side in pieces]
        tile = [
            jnp.concatenate([p.reshape(occ, -1, aux) for p in side], axis=1).reshape(occ * there, aux)
            for side in chosen
        ]
        terms = tile_plain(rows, tile, energies, sums, want, list(zip(spans, sizes)))
        windows = windows or ((0, aux),) * len(want)
        sums = [t[:, slice(*window)].astype(k) for t, k, window in zip(terms, kinds, windows)]
        return *sums, sums[0][:1, :1]
    flat_pieces = [p for side in pieces for choice in side for p in choice]
    windows = windows or ((0, aux),) * len(want)
    wide, tall = occ * there, occ * here
    summed = sums[0] is not None
    scalar = pl.BlockSpec(memory_space=pltpu.SMEM)
    vmem = pl.BlockSpec(memory_space=pltpu.VMEM)
    hbm = pl.BlockSpec(memory_space=pl.ANY)
    products = 3 if "own" in want else 2
    spreads = (2 if "own" in want else 0) + (1 if "partner" in want else 0)
    return pl.pallas_call(
        functools.partial(tile_kernel, occ, here, sizes, choices, windows, want, summed, spans),
        in_specs=[scalar, scalar, vmem, vmem, hbm, vmem, vmem] + [hbm] * len(flat_pieces) + [vmem] * (len(want) * summed),
        out_specs=[vmem] * (len(want) + 1),
        out_shape=[
            pltpu.VMEM((tall, aux), kind) if kind == jnp.float32
            else jax.ShapeDtypeStruct((tall, window[1] - window[0]), kind)
            for kind, window in zip(kinds, windows)
        ] + [jax.ShapeDtypeStruct((8, LANES), jnp.float32)],
        input_output_aliases={
            7 + len(flat_pieces) + n: n for n, kind in enumerate(kinds)
            if summed and kind == jnp.float32 and not keep
        },
        scratch_shapes=[
            pltpu.VMEM((2 * wide, aux), jnp.bfloat16),
            pltpu.VMEM((wide, tall), jnp.float32),
            pltpu.VMEM((wide, tall), jnp.float32),
            pltpu.VMEM((wide, tall), jnp.float32),
            pltpu.VMEM((tall, spreads * wide), jnp.bfloat16),
            pltpu.SemaphoreType.DMA((2 * len(sizes) * occ,)),
        ],
        compiler_params=pltpu.CompilerParams(vmem_limit_bytes=VMEM_BYTES),
        cost_estimate=pl.CostEstimate(flops=0, bytes_accessed=0, transcendentals=0),
    )(
        *energies, after, *rows, *flat_pieces, *(sums if summed else ()),
    )


def finish_kernel(window, begins, own, *refs):
    backs, (out, scratch, sem) = refs[:len(begins)], refs[-3:]
    tall, width = scratch.shape
    strip = tall // sem.shape[0]
    copies = []
    for n in range(sem.shape[0]):
        at = slice(n * strip, (n + 1) * strip)
        total = own[at, window[0]:window[1]]
        for back, begin in zip(backs, begins):
            start = window[0] - begin
            total = total + back[at, start:start + width].astype(jnp.float32)
        scratch[at] = total.astype(scratch.dtype)
        copies.append(pltpu.make_async_copy(scratch.at[at], out.at[at, pl.ds(window[0], width)], sem.at[n]))
        copies[-1].start()
    for copy in copies:
        copy.wait()


def finished(own, backs, windows):
    tall, aux = own.shape
    if tall % LANES:
        return sum((back.astype(jnp.float32) for back, _ in backs), start=own).astype(jnp.bfloat16)
    out = None
    vmem, hbm = pl.BlockSpec(memory_space=pltpu.VMEM), pl.BlockSpec(memory_space=pl.ANY)
    for window in windows:
        near = [(back, span[0]) for back, span in backs if span[0] <= window[0] and window[1] <= span[1]]
        done = [] if out is None else [out]
        out = pl.pallas_call(
            functools.partial(finish_kernel, window, [begin for _, begin in near]),
            in_specs=[vmem] * (1 + len(near)) + [hbm] * len(done),
            out_specs=hbm,
            out_shape=jax.ShapeDtypeStruct((tall, aux), jnp.bfloat16),
            input_output_aliases={1 + len(near): 0} if done else {},
            scratch_shapes=[
                pltpu.VMEM((tall, window[1] - window[0]), jnp.bfloat16),
                pltpu.SemaphoreType.DMA((4,)),
            ],
            compiler_params=pltpu.CompilerParams(vmem_limit_bytes=VMEM_BYTES),
            cost_estimate=pl.CostEstimate(flops=0, bytes_accessed=0, transcendentals=0),
        )(own, *(back for back, _ in near), *done)
    return out


def local(three_index, occ_energy, virt_energy):
    occ, here, aux = three_index.shape
    steps = lax.axis_size("virt")
    me = lax.axis_index("virt")
    sizes = (here // 2,) * 2 if here % LANES == 0 else (here,)
    offsets = [sum(sizes[:c]) for c in range(len(sizes))]
    energy_part = shifted(occ_energy, "blk", 1)
    virt_rows = lax.dynamic_slice_in_dim(virt_energy, me * here, here, 0)
    own_rows = three_index.reshape(occ * here, aux)
    part_rows = shifted(own_rows, "blk", 1)
    rows = (own_rows, part_rows)
    both = ("own", "partner")

    energies = (occ_energy, energy_part, virt_rows[None, :], virt_energy[:, None])
    done = jnp.zeros((1, 1), jnp.float32)

    def terms(runs, pieces, sums, want, after, kinds=None, windows=None, keep=False):
        after, _ = lax.optimization_barrier((done, after))
        spans = [(step, offsets[c]) for step, c in runs]
        *sums, end = tile_terms(rows, pieces, energies, sums, want, spans, after, kinds, windows, keep)
        return sums, end

    tiles = lax.optimization_barrier([
        three_index[:, o:o + size].reshape(occ * size, aux) for o, size in zip(offsets, sizes)
    ])
    ordered = lax.axis_size("blk") % 2 == 0 and len(sizes) == 2 and steps > 2
    moving = [shifted(tile, "virt", 1) for tile in tiles]
    count = len(sizes)
    waiting, runs = ([own_rows], [part_rows]), [(0, 0)]
    sums = (None, None)
    for step in range(1, steps - ordered):
        tiles, later, parts = [], [], []
        for c, tile in enumerate(moving):
            tile, *_ = lax.optimization_barrier((tile, done, *(parts or waiting[1])[-1:]))
            tiles.append(tile)
            if step < steps - 1 - ordered:
                later.append(shifted(tile, "virt", 1))
            elif ordered:
                later.append(around(tile, 1))
            parts.append(shifted(tile, "blk", 1))
            if c == 0:
                sums, done = terms(runs, waiting, sums, both, tile)
            elif ordered and step == steps - 2:
                sums, done = terms([(step, 0)], (tiles[:1], parts[:1]), sums, both, tile)
        waiting, moving, runs = (tiles, parts), later, [(step, c) for c in range(count)]
    step = steps - 1
    if ordered:
        first, second = moving
        first, *_ = lax.optimization_barrier((first, done, parts[1]))
        crossed = [passed(first, 1, 1)]
        sums, done = terms([(step - 1, 1)], (tiles[1:], parts[1:]), sums, both, first)
        held, _ = lax.optimization_barrier((tiles[0], first))
        kept, _ = lax.optimization_barrier((tiles[1], first))
        behind = [around(held, 0), around(kept, 0)]
        second, _ = lax.optimization_barrier((second, crossed[0]))
        crossed.append(passed(second, 1, 1))
        ahead, windows, runs = [first, second], ((0, aux),), [(step, 0), (step, 1)]
        ready, done = terms(runs[:1], (behind[:1], crossed[:1]), sums[1:], ("partner",), done, keep=True)
        (partner,), done = terms(
            runs[1:], (behind[1:], crossed[1:]), ready, ("partner",), done, (jnp.bfloat16,)
        )
        backs = [(passed(partner, 0, -1), windows[0])]
        late, _ = lax.optimization_barrier((behind[1], done))
        beside = [passed(behind[0], 0, 1), passed(late, 0, 1)]
        (partner,), done = terms(runs, (ahead, beside), sums[1:], ("partner",), done, (jnp.bfloat16,))
        backs.append((passed(partner, 1, -1), windows[0]))
        tail = (list(zip(behind, ahead)), list(zip(crossed, beside)))
    else:
        windows, tail = [(0, aux)], waiting
        (partner,), done = terms(runs, tail, sums[1:], ("partner",), done, (jnp.bfloat16,))
        backs = [(shifted(partner, "blk", -1), windows[0])]
    (own,), done = terms(runs, tail, sums[:1], ("own",), done)
    return finished(own, backs, windows).reshape(occ, here, aux)


def solution(mesh):
    placed = (P(("copies", "blk"), "virt", None), P(("copies", "blk")), P("copies"))
    return jax.shard_map(
        local,
        mesh=mesh,
        in_specs=placed,
        out_specs=P(("copies", "blk"), "virt", None),
        check_vma=False,
    )
```
